512 devices in a mesh: attn: 32 (over x, z_lo, core), ffn: 4 (over z_hi), grp: 4 (over y).
Axes of the slice: x: 4, y: 4, z: 16 (z_hi: 4, z_lo: 4; z = z_hi * 4 + z_lo), core: 2. Of those that a mesh axis runs over, the one named last changes fastest.
Arguments:
- layer_in: bfloat16 [64, 8192], P(None, 'attn'), may hold values from -0.59765625 to 0.59765625
- gain_attn: float32 [8192], P('attn'), may hold values from 0.1 to 1.9
- gain_ffn: float32 [8192], P('attn'), may hold values from 0.1 to 1.9
- w_query: bfloat16 [8192, 8192], P('attn', ('ffn', 'grp')), may hold values from -0.0625 to 0.0625
- w_keyval: bfloat16 [8192, 4, 256], P('attn', 'ffn'), may hold values from -4 to 4
- w_out: bfloat16 [8192, 8192], P(('ffn', 'grp'), 'attn'), may hold values from -0.0625 to 0.0625
- w_gate_up: bfloat16 [8192, 2, 26624], P('attn', None, ('ffn', 'grp')), may hold values from -0.0625 to 0.0625
- w_down: bfloat16 [26624, 8192], P(('ffn', 'grp'), 'attn'), may hold values from -0.0390625 to 0.0390625
- cache: bfloat16 [64, 4, 4096, 256], P('attn', 'ffn', 'grp'), may hold values from -200 to 200
- cache_len: int32 [64], replicated, may hold values from 512 to 4096, as said below
- request_slot: int32 [64], replicated, may hold values from 0 to 63, each once
Outputs:
- layer_out: bfloat16 [64, 8192], P(None, 'attn')
The draws below stay inside these ranges and needn't reach their ends.
Inputs may be any that keep to these rules, and one draw needn't show every extreme that they name: `cache_len`: at least 512; some request holds exactly 4096.
All inputs are finite; a program needn't handle non-finite values.
Results may differ from the reference program's by a relative error of at most 0.022.
The reference program's roundings to bfloat16 on the way (of `normed`, `queries`, `weights`, `attended`, `middle`, `normed_ffn` and `active`) count: a program that leaves them out, or rounds other values in their place, can miss the bound.
Values may be sent and summed in bfloat16 or wider, within the bound.
No kernel may reach another device: no remote copies, remote signals or barrier semaphores. Data moves between devices by JAX's collectives and lax.ppermute only.
A program may use at most 64 MiB of HBM per device.

```python
import jax
import jax.numpy as jnp
from jax import lax

D = 8192
HQ = 64
HK = 4
HD = 128
FF = 26624
LEN = 4096
GROUP = 16
REQUESTS = 64


def draw_cache(key, part):
    key = jax.random.fold_in(key, 11)
    keys_list = jax.random.split(key, 8)
    shape = (REQUESTS, HK, LEN, 2 * HD)
    head_scale = jnp.exp(jax.random.uniform(keys_list[0], (REQUESTS, HK, 1, 1), jnp.float32, -0.693, 1.099))
    base = jax.random.normal(keys_list[2], shape, jnp.float32)
    key_base = base[..., :HD] * head_scale
    value_base = base[..., HD:]
    strength = jax.random.uniform(keys_list[3], (REQUESTS, HK, 1, 1), jnp.float32, 0.7, 1.5) * 60.0
    strong = jax.random.normal(keys_list[4], (REQUESTS, HK, LEN, HD), jnp.float32) * strength
    nearby = jnp.roll(strong, 1, axis=2) + jax.random.normal(keys_list[5], (REQUESTS, HK, LEN, HD), jnp.float32)
    offset = jax.random.randint(keys_list[6], (REQUESTS, HK, 1, 1), 0, 7)
    picked = jax.random.randint(keys_list[7], (REQUESTS, HK, 1, 1), 0, 4) == 0
    first_pair = (jnp.arange(REQUESTS)[:, None, None, None] == 0) & (jnp.arange(HK)[None, :, None, None] == 0)
    picked = picked | first_pair
    slot_index = jnp.arange(LEN, dtype=jnp.int32)[None, None, :, None]
    marked = (slot_index % 8 == offset) & picked
    after = (slot_index % 8 == offset + 1) & picked
    key_part = jnp.where(marked, strong, jnp.where(after, nearby, key_base))
    result = jnp.concatenate([key_part, value_base], -1)
    return jnp.clip(result, -200.0, 200.0).astype(jnp.bfloat16)


def draw_cache_len(key, part):
    key = jax.random.fold_in(key, 12)
    first, second = jax.random.split(key)
    lengths = jax.random.randint(first, (REQUESTS,), LEN // 8, LEN + 1)
    chosen = jax.random.randint(second, (), 0, REQUESTS)
    return jnp.where(jnp.arange(REQUESTS) == chosen, LEN, lengths).astype(jnp.int32)


def draw_w_keyval(key, part):
    key = jax.random.fold_in(key, 13)
    first = jax.random.fold_in(key, 0)
    shape = (D, HK, 2 * HD)
    column = jnp.arange(2 * HD)[None, None, :]
    factor = jnp.where(column < HD, 6.0, 1.0) * D ** (-0.5)
    base = jax.random.normal(first, shape, jnp.float32)
    return jnp.clip(base * factor, -4.0, 4.0).astype(jnp.bfloat16)


def block_levels(own_key, shape, pieces, least, high):
    def one(dim, blocks):
        heights = jax.random.uniform(jax.random.fold_in(jax.random.fold_in(own_key, 6), dim), (blocks,), jnp.float32, least / len(pieces), high / len(pieces))
        return jnp.repeat(jnp.exp(heights), shape[dim] // blocks).reshape((-1,) + (1,) * (len(shape) - dim - 1))

    level = one(*pieces[0])
    for cut in pieces[1:]:
        level = level * one(*cut)
    return level


def centred(own_key, dims, scale, reach, pieces=(), kind=jnp.bfloat16):
    values = jax.random.normal(own_key, dims, jnp.float32) * scale
    if len(pieces) > 0:
        values = block_levels(own_key, dims, pieces, -0.22, 0.18) * values
    return jnp.clip(values, min=-reach, max=reach).astype(kind)


def setup_inputs(seed: int = 0) -> dict:
    streams_of = jax.random.split(jax.random.key(seed), 12)
    return {
        "layer_in": centred(streams_of[0], (REQUESTS, D), 0.1, 0.59765625, ((1, 32),)),
        "gain_attn": jnp.clip(1.0 + 0.18 * jax.random.normal(streams_of[1], (D,), jnp.float32), 0.1, 1.9),
        "gain_ffn": jnp.clip(1.0 + 0.18 * jax.random.normal(streams_of[2], (D,), jnp.float32), 0.1, 1.9),
        "w_query": centred(streams_of[3], (D, HQ * HD), D ** -0.5, 0.0625, ((0, 32), (1, 16))),
        "w_keyval": draw_w_keyval(jax.random.fold_in(streams_of[11], 71), 0),
        "w_out": centred(streams_of[5], (HQ * HD, D), (HQ * HD) ** -0.5, 0.0625, ((0, 16), (1, 32))),
        "w_gate_up": centred(streams_of[6], (D, 2, FF), D ** -0.5, 0.0625, ((0, 32), (2, 16))),
        "w_down": centred(streams_of[7], (FF, D), FF ** -0.5, 0.0390625, ((0, 16), (1, 32))),
        "cache": draw_cache(jax.random.fold_in(streams_of[11], 71), 0),
        "cache_len": draw_cache_len(jax.random.fold_in(streams_of[11], 71), 0),
        "request_slot": jax.random.permutation(streams_of[10], REQUESTS).astype(jnp.int32),
    }


def rotate(values, position):
    half = values.shape[-1] // 2
    freqs = 500000.0 ** (-(jnp.arange(half, dtype=jnp.float32) * 2.0 / values.shape[-1]))
    angles = position[:, None] * freqs[None, :]
    cosine = jnp.cos(angles)[:, None, :]
    sine = jnp.sin(angles)[:, None, :]
    first = values[..., :half]
    second = values[..., half:]
    return jnp.concatenate([first * cosine - second * sine, second * cosine + first * sine], -1)

def rms_normed(values, gain):
    return values * lax.rsqrt(lax.optimization_barrier(jnp.mean(values * values, -1, keepdims=True)) + 1e-05) * gain

def reference(layer_in, gain_attn, gain_ffn, w_query, w_keyval, w_out, w_gate_up, w_down, cache, cache_len, request_slot):
    resid = layer_in.astype(jnp.float32)
    normed = rms_normed(resid, gain_attn).astype(jnp.bfloat16)
    position = cache_len.astype(jnp.float32)
    queries = jnp.dot(normed, w_query, preferred_element_type=jnp.float32).reshape(REQUESTS, HQ, HD)
    queries = rotate(queries, position).astype(jnp.bfloat16)
    fresh = jnp.dot(normed, w_keyval.reshape(D, HK * 2 * HD), preferred_element_type=jnp.float32)
    fresh = fresh.reshape(REQUESTS, HK, 2 * HD)
    new_keys = rotate(fresh[..., :HD], position).astype(jnp.bfloat16)
    new_values = fresh[..., HD:].astype(jnp.bfloat16)
    scale = HD ** (-0.5)

    def attend(item):
        query, new_key, new_value, slot, length = item
        block = lax.dynamic_index_in_dim(cache, slot, 0, keepdims=False)
        keys_here = block[..., :HD].astype(jnp.float32)
        values_here = block[..., HD:].astype(jnp.float32)
        grouped = query.reshape(HK, GROUP, HD).astype(jnp.float32)
        scores = jnp.einsum('hgd,hjd->hgj', grouped, keys_here) * scale
        valid = (jnp.arange(LEN) < length)[None, None, :]
        scores = jnp.where(valid, scores, -1e+30)
        own = jnp.einsum('hgd,hd->hg', grouped, new_key.astype(jnp.float32)) * scale
        top = jnp.maximum(lax.optimization_barrier(jnp.max(scores, -1)), own)
        weights = jnp.where(valid, jnp.exp(scores - top[..., None]), 0.0)
        own_weight = jnp.exp(own - top)
        total = lax.optimization_barrier(jnp.sum(weights, -1)) + own_weight
        rounded = lax.optimization_barrier(weights.astype(jnp.bfloat16)).astype(jnp.float32)
        mixed = jnp.einsum('hgj,hjd->hgd', rounded, values_here)
        mixed = mixed + own_weight[..., None] * new_value.astype(jnp.float32)[:, None, :]
        return (mixed / total[..., None]).reshape(HQ * HD).astype(jnp.bfloat16)
    attended = lax.map(attend, (queries, new_keys, new_values, request_slot, cache_len))
    projected = jnp.dot(attended, w_out, preferred_element_type=jnp.float32)
    middle = (resid + projected).astype(jnp.bfloat16)
    middle_float = middle.astype(jnp.float32)
    normed_ffn = rms_normed(middle_float, gain_ffn).astype(jnp.bfloat16)
    both = jnp.dot(normed_ffn, w_gate_up.reshape(D, 2 * FF), preferred_element_type=jnp.float32)
    both = both.reshape(REQUESTS, 2, FF)
    active = (jax.nn.silu(both[:, 0]) * both[:, 1]).astype(jnp.bfloat16)
    return (middle_float + jnp.dot(active, w_down, preferred_element_type=jnp.float32)).astype(jnp.bfloat16)
```

```python
import jax
import jax.numpy as jnp
from jax import lax
from jax.sharding import PartitionSpec as P

D = 8192
F32 = jnp.float32
BF16 = jnp.bfloat16


def exchange(parts, axis):
    return lax.all_to_all(parts, axis, 0, 0)


def spread(part, axis):
    count = lax.axis_size(axis)
    return exchange(jnp.broadcast_to(part[None], (count,) + part.shape), axis)


def rotate(values, position):
    half = values.shape[-1] // 2
    freqs = 500000.0 ** (-(jnp.arange(half, dtype=F32) * 2.0 / values.shape[-1]))
    angles = position[:, None] * freqs[None, :]
    cosine = jnp.cos(angles)[:, None, :]
    sine = jnp.sin(angles)[:, None, :]
    first = values[..., :half]
    second = values[..., half:]
    return jnp.concatenate([first * cosine - second * sine, second * cosine + first * sine], -1)


def dot(a, b):
    return jnp.dot(a, b, preferred_element_type=F32)


def sum_everywhere(part):
    over_grp = jnp.sum(spread(part.astype(BF16), "grp").astype(F32), 0)
    return jnp.sum(spread(over_grp.astype(BF16), "ffn").astype(F32), 0)


def shards(
    layer_in,
    gain_attn,
    gain_ffn,
    w_query,
    w_keyval,
    w_out,
    w_gate_up,
    w_down,
    cache,
    cache_len,
    request_slot,
):
    requests = layer_in.shape[0]
    req_here = cache.shape[0]
    slots_here = cache.shape[2]
    head_size = cache.shape[3] // 2
    query_cols = w_query.shape[1]
    heads_mine = query_cols // head_size
    attn_count = lax.axis_size("attn")
    grp_count = lax.axis_size("grp")
    heads_all = heads_mine * grp_count
    scale = head_size ** (-0.5)
    order = jnp.arange(requests, dtype=jnp.int32)
    matches = request_slot[None, :] == order[:, None]
    slot_length = jnp.sum(jnp.where(matches, cache_len[None, :], 0), axis=1)
    to_slots = matches.astype(BF16)
    to_requests = (request_slot[:, None] == order[None, :]).astype(BF16)

    resid = layer_in.astype(F32)
    squares = jnp.sum(resid * resid, axis=1)
    squares = jnp.sum(spread(squares[None], "attn"), (0, 1))
    normed = (resid * lax.rsqrt(squares / D + 1e-05)[:, None] * gain_attn).astype(BF16)
    normed = dot(to_slots, normed).astype(BF16)
    weights = jnp.concatenate([w_query, w_keyval.reshape(w_keyval.shape[0], -1)], 1)
    packed = dot(normed, weights)
    summed = jnp.sum(exchange(packed.reshape(attn_count, req_here, -1), "attn"), 0)
    my_length = lax.dynamic_slice_in_dim(
        slot_length, lax.axis_index("attn") * req_here, req_here, 0
    )
    position = my_length.astype(F32)
    queries = rotate(summed[:, :query_cols].reshape(req_here, heads_mine, head_size), position)
    queries = queries.astype(BF16)
    new_key = rotate(summed[:, None, query_cols : query_cols + head_size], position).astype(BF16)
    new_value = summed[:, query_cols + head_size : query_cols + 2 * head_size].astype(BF16)
    all_queries = spread(queries.reshape(req_here, query_cols), "grp")
    grouped = all_queries.reshape(grp_count, req_here, heads_mine, head_size)
    grouped = jnp.swapaxes(grouped, 0, 1).reshape(req_here, heads_all, head_size)

    keys_here = cache[:, 0, :, :head_size]
    values_here = cache[:, 0, :, head_size:]
    scores = jnp.einsum("rgd,rjd->rgj", grouped, keys_here, preferred_element_type=F32) * scale
    positions = lax.axis_index("grp") * slots_here + jnp.arange(slots_here, dtype=jnp.int32)
    valid = (positions[None, :] < my_length[:, None])[:, None, :]
    scores = jnp.where(valid, scores, -1e30)
    top = jnp.max(scores, -1)
    weights = jnp.where(valid, jnp.exp(scores - top[..., None]), 0.0)
    total = jnp.sum(weights, -1)
    mixed = jnp.einsum(
        "rgj,rjd->rgd", weights.astype(BF16), values_here, preferred_element_type=F32
    )
    half = (req_here, heads_all, head_size // 2)
    packed = jnp.concatenate(
        [mixed, jnp.broadcast_to(top[..., None], half), jnp.broadcast_to(total[..., None], half)],
        -1,
    )
    packed = packed.reshape(req_here, grp_count, heads_mine, 2 * head_size)
    packed = exchange(jnp.swapaxes(packed, 0, 1), "grp")
    mixed = packed[..., :head_size]
    top = packed[..., head_size]
    total = packed[..., head_size + head_size // 2]
    own = jnp.sum(queries.astype(F32) * new_key.astype(F32), -1) * scale
    best = jnp.maximum(jnp.max(top, 0), own)
    factor = jnp.exp(top - best)
    own_weight = jnp.exp(own - best)
    denom = jnp.sum(total * factor, 0) + own_weight
    attended = jnp.sum(mixed * factor[..., None], 0)
    attended = attended + own_weight[..., None] * new_value.astype(F32)[:, None, :]
    attended = (attended / denom[..., None]).astype(BF16).reshape(req_here, query_cols)
    attended = spread(attended, "attn").reshape(requests, query_cols)
    attended = dot(to_requests, attended).astype(BF16)
    middle = (resid + sum_everywhere(dot(attended, w_out))).astype(BF16)

    middle_float = middle.astype(F32)
    squares = jnp.sum(middle_float * middle_float, axis=1)
    squares_high = squares.astype(BF16)
    squares_low = (squares - squares_high.astype(F32)).astype(BF16)
    half = (requests, 64)
    units = w_gate_up.shape[2]
    both = dot((middle_float * gain_ffn).astype(BF16), w_gate_up.reshape(w_gate_up.shape[0], -1))
    packed = jnp.concatenate(
        [
            both.astype(BF16),
            jnp.broadcast_to(squares_high[:, None], half),
            jnp.broadcast_to(squares_low[:, None], half),
        ],
        1,
    )
    packed = exchange(packed.reshape(attn_count, req_here, -1), "attn").astype(F32)
    summed = jnp.sum(packed, 0)
    squares = summed[:, 2 * units] + summed[:, 2 * units + 64]
    summed = summed * lax.rsqrt(squares / D + 1e-05)[:, None]
    active = (jax.nn.silu(summed[:, :units]) * summed[:, units : 2 * units]).astype(BF16)
    active = spread(active, "attn").reshape(requests, units)
    return (middle_float + sum_everywhere(dot(active, w_down))).astype(BF16)


def solution(mesh):
    placed = (
        P(None, "attn"),
        P("attn"),
        P("attn"),
        P("attn", ("ffn", "grp")),
        P("attn", "ffn", None),
        P(("ffn", "grp"), "attn"),
        P("attn", None, ("ffn", "grp")),
        P(("ffn", "grp"), "attn"),
        P("attn", "ffn", "grp", None),
        P(),
        P(),
    )
    return jax.shard_map(
        shards, mesh=mesh, in_specs=placed, out_specs=P(None, "attn"), check_vma=False
    )
```

```python
import jax
import jax.numpy as jnp
from jax import lax
from jax.sharding import PartitionSpec as P

D = 8192
F32 = jnp.float32
BF16 = jnp.bfloat16


def exchange(parts, axis):
    return lax.all_to_all(parts, axis, 0, 0)


def spread(part, axis):
    count = lax.axis_size(axis)
    return exchange(jnp.broadcast_to(part[None], (count,) + part.shape), axis)


def angles(position, size):
    half = size // 2
    freqs = 500000.0 ** (-(jnp.arange(half, dtype=F32) * 2.0 / size))
    turned = position[:, None] * freqs[None, :]
    return jnp.cos(turned)[:, None, :], jnp.sin(turned)[:, None, :]


def rotate(values, cosine, sine):
    half = values.shape[-1] // 2
    first = values[..., :half]
    second = values[..., half:]
    return jnp.concatenate([first * cosine - second * sine, second * cosine + first * sine], -1)


def dot(a, b):
    return jnp.dot(a, b, preferred_element_type=F32)


def sum_everywhere(part):
    over_grp = jnp.sum(spread(part.astype(BF16), "grp").astype(F32), 0)
    return jnp.sum(spread(over_grp.astype(BF16), "ffn").astype(F32), 0)


def shards(
    layer_in,
    gain_attn,
    gain_ffn,
    w_query,
    w_keyval,
    w_out,
    w_gate_up,
    w_down,
    cache,
    cache_len,
    request_slot,
):
    requests = layer_in.shape[0]
    req_here = cache.shape[0]
    slots_here = cache.shape[2]
    head_size = cache.shape[3] // 2
    query_cols = w_query.shape[1]
    heads_mine = query_cols // head_size
    attn_count = lax.axis_size("attn")
    grp_count = lax.axis_size("grp")
    heads_all = heads_mine * grp_count
    scale = head_size ** (-0.5)
    order = jnp.arange(requests, dtype=jnp.int32)
    matches = request_slot[None, :] == order[:, None]
    slot_rows = dot(matches.astype(BF16), layer_in)
    squares = jnp.sum(slot_rows * slot_rows, axis=1)
    squares = spread(squares[None], "attn")

    slot_length = jnp.sum(jnp.where(matches, cache_len[None, :], 0), axis=1)
    my_length = lax.dynamic_slice_in_dim(
        slot_length, lax.axis_index("attn") * req_here, req_here, 0
    )
    cosine, sine = angles(my_length.astype(F32), head_size)
    positions = lax.axis_index("grp") * slots_here + jnp.arange(slots_here, dtype=jnp.int32)
    valid = (positions[None, :] < my_length[:, None])[:, None, :]
    share = 2 * head_size // grp_count
    keyval_share = lax.dynamic_slice_in_dim(
        w_keyval[:, 0, :], lax.axis_index("grp") * share, share, 1
    )
    weights = jnp.concatenate([w_query, keyval_share], 1)
    gate_up = w_gate_up.reshape(w_gate_up.shape[0], -1)
    squares, cosine, sine, valid, weights, gate_up, slot_rows = lax.optimization_barrier(
        (squares, cosine, sine, valid, weights, gate_up, slot_rows)
    )
    squares = jnp.sum(squares, (0, 1))
    normed = (slot_rows * lax.rsqrt(squares / D + 1e-05)[:, None] * gain_attn).astype(BF16)
    packed = dot(normed, weights)
    summed = jnp.sum(exchange(packed.reshape(attn_count, req_here, -1), "attn"), 0)
    queries = rotate(
        summed[:, :query_cols].reshape(req_here, heads_mine, head_size), cosine, sine
    )
    queries = queries.astype(BF16)
    sent = jnp.concatenate(
        [queries.astype(F32).reshape(req_here, query_cols), summed[:, query_cols:]], 1
    )
    arrived = spread(sent, "grp")
    fresh = jnp.swapaxes(arrived[..., query_cols:], 0, 1).reshape(req_here, 2 * head_size)
    new_key = rotate(fresh[:, None, :head_size], cosine, sine).astype(BF16)
    new_value = fresh[:, head_size:].astype(BF16)
    own = jnp.sum(queries.astype(F32) * new_key.astype(F32), -1) * scale
    all_queries = arrived[..., :query_cols].astype(BF16)
    new_value, own, all_queries = lax.optimization_barrier((new_value, own, all_queries))
    grouped = all_queries.reshape(grp_count, req_here, heads_mine, head_size)
    grouped = jnp.swapaxes(grouped, 0, 1).reshape(req_here, heads_all, head_size)

    keys_here = cache[:, 0, :, :head_size]
    values_here = cache[:, 0, :, head_size:]
    scores = jnp.einsum("rgd,rjd->rgj", grouped, keys_here, preferred_element_type=F32) * scale
    scores = jnp.where(valid, scores, -1e30)
    top = jnp.max(scores, -1)
    weights = jnp.where(valid, jnp.exp(scores - top[..., None]), 0.0)
    total = jnp.sum(weights, -1)
    mixed = jnp.einsum(
        "rgj,rjd->rgd", weights.astype(BF16), values_here, preferred_element_type=F32
    )
    half = (req_here, heads_all, head_size // 2)
    packed = jnp.concatenate(
        [mixed, jnp.broadcast_to(top[..., None], half), jnp.broadcast_to(total[..., None], half)],
        -1,
    )
    packed = packed.reshape(req_here, grp_count, heads_mine, 2 * head_size)
    packed = exchange(jnp.swapaxes(packed, 0, 1), "grp")
    mixed = packed[..., :head_size]
    top = packed[..., head_size]
    total = packed[..., head_size + head_size // 2]
    best = jnp.maximum(jnp.max(top, 0), own)
    factor = jnp.exp(top - best)
    own_weight = jnp.exp(own - best)
    denom = jnp.sum(total * factor, 0) + own_weight
    attended = jnp.sum(mixed * factor[..., None], 0)
    attended = attended + own_weight[..., None] * new_value.astype(F32)[:, None, :]
    attended = (attended / denom[..., None]).astype(BF16).reshape(req_here, query_cols)
    attended = spread(attended, "attn").reshape(requests, query_cols)
    to_requests = (request_slot[:, None] == order[None, :]).astype(BF16)
    attended = dot(to_requests, attended).astype(BF16)
    resid = layer_in.astype(F32)
    middle = (resid + sum_everywhere(dot(attended, w_out))).astype(BF16)

    middle_float = middle.astype(F32)
    squares = jnp.sum(middle_float * middle_float, axis=1)
    squares_high = squares.astype(BF16)
    squares_low = (squares - squares_high.astype(F32)).astype(BF16)
    half = (requests, 64)
    units = w_gate_up.shape[2]
    both = dot((middle_float * gain_ffn).astype(BF16), gate_up)
    packed = jnp.concatenate(
        [
            both.astype(BF16),
            jnp.broadcast_to(squares_high[:, None], half),
            jnp.broadcast_to(squares_low[:, None], half),
        ],
        1,
    )
    packed = exchange(packed.reshape(attn_count, req_here, -1), "attn").astype(F32)
    summed = jnp.sum(packed, 0)
    squares = summed[:, 2 * units] + summed[:, 2 * units + 64]
    summed = summed * lax.rsqrt(squares / D + 1e-05)[:, None]
    active = (jax.nn.silu(summed[:, :units]) * summed[:, units : 2 * units]).astype(BF16)
    active = spread(active, "attn").reshape(requests, units)
    return (middle_float + sum_everywhere(dot(active, w_down))).astype(BF16)


def solution(mesh):
    placed = (
        P(None, "attn"),
        P("attn"),
        P("attn"),
        P("attn", ("ffn", "grp")),
        P("attn", "ffn", None),
        P(("ffn", "grp"), "attn"),
        P("attn", None, ("ffn", "grp")),
        P(("ffn", "grp"), "attn"),
        P("attn", "ffn", "grp", None),
        P(),
        P(),
    )
    return jax.shard_map(
        shards, mesh=mesh, in_specs=placed, out_specs=P(None, "attn"), check_vma=False
    )
```

```python
import jax
import jax.numpy as jnp
from jax import lax
from jax.sharding import PartitionSpec as P

D = 8192
F32 = jnp.float32
BF16 = jnp.bfloat16


def exchange(parts, axis):
    return lax.all_to_all(parts, axis, 0, 0)


def spread(part, axis):
    count = lax.axis_size(axis)
    return exchange(jnp.broadcast_to(part[None], (count,) + part.shape), axis)


def angles(position, size):
    half = size // 2
    freqs = 500000.0 ** (-(jnp.arange(half, dtype=F32) * 2.0 / size))
    turned = position[:, None] * freqs[None, :]
    return jnp.cos(turned)[:, None, :], jnp.sin(turned)[:, None, :]


def rotate(values, cosine, sine):
    half = values.shape[-1] // 2
    first = values[..., :half]
    second = values[..., half:]
    return jnp.concatenate([first * cosine - second * sine, second * cosine + first * sine], -1)


def dot(a, b):
    return jnp.dot(a, b, preferred_element_type=F32)


def sum_pairs(total, axis):
    for pairs in (((0, 1), (2, 3)), ((0, 3), (1, 2))):
        swaps = [(a, b) for a, b in pairs] + [(b, a) for a, b in pairs]
        mine = total.astype(BF16)
        total = mine.astype(F32) + lax.ppermute(mine, axis, swaps).astype(F32)
    return total


def sum_spread(part, axis):
    return jnp.sum(spread(part.astype(BF16), axis).astype(F32), 0)


def shards(
    layer_in,
    gain_attn,
    gain_ffn,
    w_query,
    w_keyval,
    w_out,
    w_gate_up,
    w_down,
    cache,
    cache_len,
    request_slot,
):
    requests = layer_in.shape[0]
    req_here = cache.shape[0]
    slots_here = cache.shape[2]
    head_size = cache.shape[3] // 2
    query_cols = w_query.shape[1]
    heads_mine = query_cols // head_size
    attn_count = lax.axis_size("attn")
    grp_count = lax.axis_size("grp")
    heads_all = heads_mine * grp_count
    scale = head_size ** (-0.5)
    order = jnp.arange(requests, dtype=jnp.int32)
    matches = request_slot[None, :] == order[:, None]
    slot_rows = dot(matches.astype(BF16), layer_in)
    squares = jnp.sum(slot_rows * slot_rows, axis=1)
    squares = spread(squares[None], "attn")

    slot_length = jnp.sum(jnp.where(matches, cache_len[None, :], 0), axis=1)
    my_length = lax.dynamic_slice_in_dim(
        slot_length, lax.axis_index("attn") * req_here, req_here, 0
    )
    cosine, sine = angles(my_length.astype(F32), head_size)
    positions = lax.axis_index("grp") * slots_here + jnp.arange(slots_here, dtype=jnp.int32)
    valid = (positions[None, :] < my_length[:, None])[:, None, :]
    keys_here = cache[:, 0, :, :head_size]
    values_here = cache[:, 0, :, head_size:]
    weights = jnp.concatenate([w_query, w_keyval.reshape(w_keyval.shape[0], -1)], 1)
    squares, cosine, sine, valid, keys_here, values_here, weights = lax.optimization_barrier(
        (squares, cosine, sine, valid, keys_here, values_here, weights)
    )
    squares = jnp.sum(squares, (0, 1))
    normed = (slot_rows * lax.rsqrt(squares / D + 1e-05)[:, None] * gain_attn).astype(BF16)
    packed = dot(normed, weights)
    summed = exchange(packed.reshape(attn_count, req_here, -1), "attn")
    summed = jnp.sum(summed, 0)
    queries = rotate(
        summed[:, :query_cols].reshape(req_here, heads_mine, head_size), cosine, sine
    )
    queries = queries.astype(BF16)
    new_key = rotate(summed[:, None, query_cols : query_cols + head_size], cosine, sine)
    new_key = new_key.astype(BF16)
    new_value = summed[:, query_cols + head_size :].astype(BF16).astype(F32)
    own = jnp.sum(queries.astype(F32) * new_key.astype(F32), -1) * scale
    flat_queries, new_value, own = lax.optimization_barrier(
        (queries.reshape(req_here, query_cols), new_value, own)
    )
    all_queries = spread(flat_queries, "grp")
    grouped = all_queries.reshape(grp_count, req_here, heads_mine, head_size)
    grouped = jnp.swapaxes(grouped, 0, 1).reshape(req_here, heads_all, head_size)

    scores = jnp.einsum("rgd,rjd->rgj", grouped, keys_here, preferred_element_type=F32) * scale
    scores = jnp.where(valid, scores, -1e30)
    top = jnp.max(scores, -1)
    weights = jnp.where(valid, jnp.exp(scores - top[..., None]), 0.0)
    total = jnp.sum(weights, -1)
    mixed = jnp.einsum(
        "rgj,rjd->rgd", weights.astype(BF16), values_here, preferred_element_type=F32
    )
    half = (req_here, heads_all, head_size // 2)
    packed = jnp.concatenate(
        [mixed, jnp.broadcast_to(top[..., None], half), jnp.broadcast_to(total[..., None], half)],
        -1,
    )
    packed = packed.reshape(req_here, grp_count, heads_mine, 2 * head_size)
    packed = exchange(jnp.swapaxes(packed, 0, 1), "grp")
    mixed = packed[..., :head_size]
    top = packed[..., head_size]
    total = packed[..., head_size + head_size // 2]
    best = jnp.maximum(jnp.max(top, 0), own)
    factor = jnp.exp(top - best)
    own_weight = jnp.exp(own - best)
    denom = jnp.sum(total * factor, 0) + own_weight
    attended = jnp.sum(mixed * factor[..., None], 0)
    attended = attended + own_weight[..., None] * new_value[:, None, :]
    attended = (attended / denom[..., None]).astype(BF16).reshape(req_here, query_cols)
    attended = spread(attended, "attn").reshape(requests, query_cols)
    to_requests = (request_slot[:, None] == order[None, :]).astype(BF16)
    attended = dot(to_requests, attended).astype(BF16)
    resid = layer_in.astype(F32)
    middle = (resid + sum_pairs(sum_spread(dot(attended, w_out), "grp"), "ffn")).astype(BF16)

    middle_float = middle.astype(F32)
    squares = jnp.sum(middle_float * middle_float, axis=1)
    squares_high = squares.astype(BF16)
    squares_low = (squares - squares_high.astype(F32)).astype(BF16)
    half = (requests, 64)
    units = w_gate_up.shape[2]
    both = dot((middle_float * gain_ffn).astype(BF16), w_gate_up.reshape(w_gate_up.shape[0], -1))
    packed = jnp.concatenate(
        [
            both.astype(BF16),
            jnp.broadcast_to(squares_high[:, None], half),
            jnp.broadcast_to(squares_low[:, None], half),
        ],
        1,
    )
    packed = exchange(packed.reshape(attn_count, req_here, -1), "attn").astype(F32)
    summed = jnp.sum(packed, 0)
    squares = summed[:, 2 * units] + summed[:, 2 * units + 64]
    summed = summed * lax.rsqrt(squares / D + 1e-05)[:, None]
    active = (jax.nn.silu(summed[:, :units]) * summed[:, units : 2 * units]).astype(BF16)
    active = spread(active, "attn").reshape(requests, units)
    return (middle_float + sum_pairs(sum_spread(dot(active, w_down), "grp"), "ffn")).astype(BF16)


def solution(mesh):
    placed = (
        P(None, "attn"),
        P("attn"),
        P("attn"),
        P("attn", ("ffn", "grp")),
        P("attn", "ffn", None),
        P(("ffn", "grp"), "attn"),
        P("attn", None, ("ffn", "grp")),
        P(("ffn", "grp"), "attn"),
        P("attn", "ffn", "grp", None),
        P(),
        P(),
    )
    return jax.shard_map(
        shards, mesh=mesh, in_specs=placed, out_specs=P(None, "attn"), check_vma=False
    )
```

```python
import jax
import jax.numpy as jnp
from jax import lax
from jax.sharding import PartitionSpec as P

D = 8192
F32 = jnp.float32
BF16 = jnp.bfloat16


def exchange(parts, axis):
    return lax.all_to_all(parts, axis, 0, 0)


def spread(part, axis):
    count = lax.axis_size(axis)
    return exchange(jnp.broadcast_to(part[None], (count,) + part.shape), axis)


def angles(position, size):
    half = size // 2
    freqs = 500000.0 ** (-(jnp.arange(half, dtype=F32) * 2.0 / size))
    turned = position[:, None] * freqs[None, :]
    return jnp.cos(turned)[:, None, :], jnp.sin(turned)[:, None, :]


def rotate(values, cosine, sine):
    half = values.shape[-1] // 2
    first = values[..., :half]
    second = values[..., half:]
    return jnp.concatenate([first * cosine - second * sine, second * cosine + first * sine], -1)


def dot(a, b):
    return jnp.dot(a, b, preferred_element_type=F32)


def sum_relay(part, axis, ahead, behind):
    def swap(values, pair):
        return lax.ppermute(values, axis, (pair, pair[::-1]))

    def hand(values, sources, targets):
        return lax.ppermute(values, axis, tuple(zip(sources, targets)))

    def add(one, two):
        return (one.astype(F32) + two.astype(F32)).astype(BF16)

    mine = part.astype(BF16)
    from_ahead = swap(mine, ahead)
    sum_ahead = add(mine, from_ahead)
    here = (lax.axis_index(axis) == ahead[0]) | (lax.axis_index(axis) == ahead[1])
    down = hand(jnp.pad(sum_ahead, ((0, 16), (0, 0))), ahead, behind)[: part.shape[0]]
    mine = jnp.where(here, sum_ahead, mine)
    from_behind = swap(mine, behind)
    sum_behind = add(mine, from_behind)
    up = hand(jnp.where(here, down, sum_behind), behind, ahead)
    near = jnp.where(here, sum_ahead, sum_behind)
    far = jnp.where(here, up, down)
    return near.astype(F32) + far.astype(F32)


def sum_spread(part, axis):
    return jnp.sum(spread(part.astype(BF16), axis).astype(F32), 0)


def shards(
    layer_in,
    gain_attn,
    gain_ffn,
    w_query,
    w_keyval,
    w_out,
    w_gate_up,
    w_down,
    cache,
    cache_len,
    request_slot,
):
    requests = layer_in.shape[0]
    req_here = cache.shape[0]
    slots_here = cache.shape[2]
    head_size = cache.shape[3] // 2
    query_cols = w_query.shape[1]
    heads_mine = query_cols // head_size
    attn_count = lax.axis_size("attn")
    grp_count = lax.axis_size("grp")
    heads_all = heads_mine * grp_count
    scale = head_size ** (-0.5)
    order = jnp.arange(requests, dtype=jnp.int32)
    matches = request_slot[None, :] == order[:, None]
    slot_rows = dot(matches.astype(BF16), layer_in)
    squares = jnp.sum(slot_rows * slot_rows, axis=1)
    squares = spread(squares[None], "attn")

    slot_length = jnp.sum(jnp.where(matches, cache_len[None, :], 0), axis=1)
    my_length = lax.dynamic_slice_in_dim(
        slot_length, lax.axis_index("attn") * req_here, req_here, 0
    )
    cosine, sine = angles(my_length.astype(F32), head_size)
    positions = lax.axis_index("grp") * slots_here + jnp.arange(slots_here, dtype=jnp.int32)
    valid = (positions[None, :] < my_length[:, None])[:, None, :]
    keys_here = cache[:, 0, :, :head_size]
    values_here = cache[:, 0, :, head_size:]
    weights = jnp.concatenate([w_query, w_keyval.reshape(w_keyval.shape[0], -1)], 1)
    squares, cosine, sine, valid, keys_here, values_here, weights = lax.optimization_barrier(
        (squares, cosine, sine, valid, keys_here, values_here, weights)
    )
    squares = jnp.sum(squares, (0, 1))
    normed = (slot_rows * lax.rsqrt(squares / D + 1e-05)[:, None] * gain_attn).astype(BF16)
    packed = dot(normed, weights)
    summed = exchange(packed.reshape(attn_count, req_here, -1), "attn")
    summed = jnp.sum(summed, 0)
    queries = rotate(
        summed[:, :query_cols].reshape(req_here, heads_mine, head_size), cosine, sine
    )
    queries = queries.astype(BF16)
    new_key = rotate(summed[:, None, query_cols : query_cols + head_size], cosine, sine)
    new_key = new_key.astype(BF16)
    new_value = summed[:, query_cols + head_size :].astype(BF16).astype(F32)
    own = jnp.sum(queries.astype(F32) * new_key.astype(F32), -1) * scale
    flat_queries, new_value, own = lax.optimization_barrier(
        (queries.reshape(req_here, query_cols), new_value, own)
    )
    all_queries = spread(flat_queries, "grp")
    grouped = all_queries.reshape(grp_count, req_here, heads_mine, head_size)
    grouped = jnp.swapaxes(grouped, 0, 1).reshape(req_here, heads_all, head_size)

    scores = jnp.einsum("rgd,rjd->rgj", grouped, keys_here, preferred_element_type=F32) * scale
    scores = jnp.where(valid, scores, -1e30)
    top = jnp.max(scores, -1)
    weights = jnp.where(valid, jnp.exp(scores - top[..., None]), 0.0)
    total = jnp.sum(weights, -1)
    mixed = jnp.einsum(
        "rgj,rjd->rgd", weights.astype(BF16), values_here, preferred_element_type=F32
    )
    half = (req_here, heads_all, head_size // 2)
    packed = jnp.concatenate(
        [mixed, jnp.broadcast_to(top[..., None], half), jnp.broadcast_to(total[..., None], half)],
        -1,
    )
    packed = packed.reshape(req_here, grp_count, heads_mine, 2 * head_size)
    packed = exchange(jnp.swapaxes(packed, 0, 1), "grp")
    mixed = packed[..., :head_size]
    top = packed[..., head_size]
    total = packed[..., head_size + head_size // 2]
    best = jnp.maximum(jnp.max(top, 0), own)
    factor = jnp.exp(top - best)
    own_weight = jnp.exp(own - best)
    denom = jnp.sum(total * factor, 0) + own_weight
    attended = jnp.sum(mixed * factor[..., None], 0)
    attended = attended + own_weight[..., None] * new_value[:, None, :]
    attended = (attended / denom[..., None]).astype(BF16).reshape(req_here, query_cols)
    attended = spread(attended, "attn").reshape(requests, query_cols)
    to_requests = (request_slot[:, None] == order[None, :]).astype(BF16)
    attended = dot(to_requests, attended).astype(BF16)
    resid = layer_in.astype(F32)
    projected = sum_spread(dot(attended, w_out), "grp")
    middle = (resid + sum_relay(projected, "ffn", (0, 1), (3, 2))).astype(BF16)

    middle_float = middle.astype(F32)
    squares = jnp.sum(middle_float * middle_float, axis=1)
    squares_high = squares.astype(BF16)
    squares_low = (squares - squares_high.astype(F32)).astype(BF16)
    half = (requests, 64)
    units = w_gate_up.shape[2]
    both = dot((middle_float * gain_ffn).astype(BF16), w_gate_up.reshape(w_gate_up.shape[0], -1))
    packed = jnp.concatenate(
        [
            both.astype(BF16),
            jnp.broadcast_to(squares_high[:, None], half),
            jnp.broadcast_to(squares_low[:, None], half),
        ],
        1,
    )
    packed = exchange(packed.reshape(attn_count, req_here, -1), "attn").astype(F32)
    summed = jnp.sum(packed, 0)
    squares = summed[:, 2 * units] + summed[:, 2 * units + 64]
    summed = summed * lax.rsqrt(squares / D + 1e-05)[:, None]
    active = (jax.nn.silu(summed[:, :units]) * summed[:, units : 2 * units]).astype(BF16)
    active = spread(active, "attn").reshape(requests, units)
    down = sum_spread(dot(active, w_down), "grp")
    return (middle_float + sum_relay(down, "ffn", (3, 2), (0, 1))).astype(BF16)


def solution(mesh):
    placed = (
        P(None, "attn"),
        P("attn"),
        P("attn"),
        P("attn", ("ffn", "grp")),
        P("attn", "ffn", None),
        P(("ffn", "grp"), "attn"),
        P("attn", None, ("ffn", "grp")),
        P(("ffn", "grp"), "attn"),
        P("attn", "ffn", "grp", None),
        P(),
        P(),
    )
    return jax.shard_map(
        shards, mesh=mesh, in_specs=placed, out_specs=P(None, "attn"), check_vma=False
    )
```

```python
import jax
import jax.numpy as jnp
from jax import lax
from jax.sharding import Mesh
from jax.sharding import PartitionSpec as P

D = 8192
F32 = jnp.float32
BF16 = jnp.bfloat16


ATTN = ("chip", "core")


def exchange(parts, axis):
    return lax.all_to_all(parts, axis, 0, 0)


def spread(part, axis):
    count = lax.psum(1, axis)
    return exchange(jnp.broadcast_to(part[None], (count,) + part.shape), axis)


def angles(position, size):
    half = size // 2
    freqs = 500000.0 ** (-(jnp.arange(half, dtype=F32) * 2.0 / size))
    turned = position[:, None] * freqs[None, :]
    return jnp.cos(turned)[:, None, :], jnp.sin(turned)[:, None, :]


def rotate(values, cosine, sine):
    half = values.shape[-1] // 2
    first = values[..., :half]
    second = values[..., half:]
    return jnp.concatenate([first * cosine - second * sine, second * cosine + first * sine], -1)


def dot(a, b):
    return jnp.dot(a, b, preferred_element_type=F32)


def sum_relay(part, axis, ahead, behind):
    def swap(values, pair):
        return lax.ppermute(values, axis, (pair, pair[::-1]))

    def hand(values, sources, targets):
        return lax.ppermute(values, axis, tuple(zip(sources, targets)))

    def add(one, two):
        return (one.astype(F32) + two.astype(F32)).astype(BF16)

    mine = part.astype(BF16)
    from_ahead = swap(mine, ahead)
    sum_ahead = add(mine, from_ahead)
    here = (lax.axis_index(axis) == ahead[0]) | (lax.axis_index(axis) == ahead[1])
    down = hand(jnp.pad(sum_ahead, ((0, 16), (0, 0))), ahead, behind)[: part.shape[0]]
    mine = jnp.where(here, sum_ahead, mine)
    from_behind = swap(mine, behind)
    sum_behind = add(mine, from_behind)
    up = hand(jnp.where(here, down, sum_behind), behind, ahead)
    near = jnp.where(here, sum_ahead, sum_behind)
    far = jnp.where(here, up, down)
    return near.astype(F32) + far.astype(F32)


def sum_spread(part, axis):
    return jnp.sum(spread(part.astype(BF16), axis).astype(F32), 0)


def shards(
    layer_in,
    gain_attn,
    gain_ffn,
    w_query,
    w_keyval,
    w_out,
    w_gate_up,
    w_down,
    cache,
    cache_len,
    request_slot,
):
    requests = layer_in.shape[0]
    req_here = cache.shape[0]
    slots_here = cache.shape[2]
    head_size = cache.shape[3] // 2
    query_cols = w_query.shape[1]
    heads_mine = query_cols // head_size
    attn_count = lax.psum(1, ATTN)
    grp_count = lax.axis_size("grp")
    heads_all = heads_mine * grp_count
    scale = head_size ** (-0.5)
    order = jnp.arange(requests, dtype=jnp.int32)
    matches = request_slot[None, :] == order[:, None]
    slot_rows = dot(matches.astype(BF16), layer_in)
    squares = jnp.sum(slot_rows * slot_rows, axis=1)
    squares = spread(squares[None], ATTN)

    slot_length = jnp.sum(jnp.where(matches, cache_len[None, :], 0), axis=1)
    my_length = lax.dynamic_slice_in_dim(
        slot_length, lax.axis_index(ATTN) * req_here, req_here, 0
    )
    cosine, sine = angles(my_length.astype(F32), head_size)
    positions = lax.axis_index("grp") * slots_here + jnp.arange(slots_here, dtype=jnp.int32)
    valid = (positions[None, :] < my_length[:, None])[:, None, :]
    keys_here = cache[:, 0, :, :head_size]
    values_here = cache[:, 0, :, head_size:]
    weights = jnp.concatenate([w_query, w_keyval.reshape(w_keyval.shape[0], -1)], 1)
    squares, cosine, sine, valid, keys_here, values_here, weights = lax.optimization_barrier(
        (squares, cosine, sine, valid, keys_here, values_here, weights)
    )
    squares = jnp.sum(squares, (0, 1))
    normed = (slot_rows * lax.rsqrt(squares / D + 1e-05)[:, None] * gain_attn).astype(BF16)
    packed = dot(normed, weights)
    summed = exchange(packed.reshape(attn_count, req_here, -1), ATTN)
    summed = jnp.sum(summed, 0)
    queries = rotate(
        summed[:, :query_cols].reshape(req_here, heads_mine, head_size), cosine, sine
    )
    queries = queries.astype(BF16)
    new_key = rotate(summed[:, None, query_cols : query_cols + head_size], cosine, sine)
    new_key = new_key.astype(BF16)
    new_value = summed[:, query_cols + head_size :].astype(BF16).astype(F32)
    own = jnp.sum(queries.astype(F32) * new_key.astype(F32), -1) * scale
    flat_queries, new_value, own = lax.optimization_barrier(
        (queries.reshape(req_here, query_cols), new_value, own)
    )
    all_queries = spread(flat_queries, "grp")
    grouped = all_queries.reshape(grp_count, req_here, heads_mine, head_size)
    grouped = jnp.swapaxes(grouped, 0, 1).reshape(req_here, heads_all, head_size)

    scores = jnp.einsum("rgd,rjd->rgj", grouped, keys_here, preferred_element_type=F32) * scale
    scores = jnp.where(valid, scores, -1e30)
    top = jnp.max(scores, -1)
    weights = jnp.where(valid, jnp.exp(scores - top[..., None]), 0.0)
    total = jnp.sum(weights, -1)
    mixed = jnp.einsum(
        "rgj,rjd->rgd", weights.astype(BF16), values_here, preferred_element_type=F32
    )
    half = (req_here, heads_all, head_size // 2)
    packed = jnp.concatenate(
        [mixed, jnp.broadcast_to(top[..., None], half), jnp.broadcast_to(total[..., None], half)],
        -1,
    )
    packed = packed.reshape(req_here, grp_count, heads_mine, 2 * head_size)
    packed = exchange(jnp.swapaxes(packed, 0, 1), "grp")
    mixed = packed[..., :head_size]
    top = packed[..., head_size]
    total = packed[..., head_size + head_size // 2]
    best = jnp.maximum(jnp.max(top, 0), own)
    factor = jnp.exp(top - best)
    own_weight = jnp.exp(own - best)
    denom = jnp.sum(total * factor, 0) + own_weight
    attended = jnp.sum(mixed * factor[..., None], 0)
    attended = attended + own_weight[..., None] * new_value[:, None, :]
    attended = (attended / denom[..., None]).astype(BF16).reshape(req_here, query_cols)
    attended = spread(attended, ATTN).reshape(requests, query_cols)
    to_requests = (request_slot[:, None] == order[None, :]).astype(BF16)
    attended = dot(to_requests, attended).astype(BF16)
    resid = layer_in.astype(F32)
    projected = sum_spread(dot(attended, w_out), "grp")
    middle = (resid + sum_relay(projected, "ffn", (0, 1), (3, 2))).astype(BF16)

    middle_float = middle.astype(F32)
    squares = jnp.sum(middle_float * middle_float, axis=1)
    squares_high = squares.astype(BF16)
    squares_low = (squares - squares_high.astype(F32)).astype(BF16)
    units = w_gate_up.shape[2]
    both = dot((middle_float * gain_ffn).astype(BF16), w_gate_up.reshape(w_gate_up.shape[0], -1))
    core = lax.axis_index("core")
    lane = jnp.arange(128, dtype=jnp.int32)[None, :]
    tail = jnp.where(lane % 64 < 32, squares_high[:, None], squares_low[:, None])
    tail = jnp.where(lane // 64 == core, tail, jnp.zeros((), BF16))
    packed = jnp.concatenate([both.astype(BF16), tail], 1)
    packed = packed.reshape(attn_count // 2, 2, req_here, -1)
    kept = lax.dynamic_index_in_dim(packed, core, 1, False)
    given = lax.dynamic_index_in_dim(packed, 1 - core, 1, False)
    pair = kept.astype(F32) + lax.ppermute(given, "core", ((0, 1), (1, 0))).astype(F32)
    packed = exchange(pair.astype(BF16), "chip").astype(F32)
    summed = jnp.sum(packed, 0)
    squares = sum(summed[:, 2 * units + start] for start in (0, 32, 64, 96))
    summed = summed * lax.rsqrt(squares / D + 1e-05)[:, None]
    active = (jax.nn.silu(summed[:, :units]) * summed[:, units : 2 * units]).astype(BF16)
    active = spread(active, ATTN).reshape(requests, units)
    down = sum_spread(dot(active, w_down), "grp")
    return (middle_float + sum_relay(down, "ffn", (3, 2), (0, 1))).astype(BF16)


def solution(mesh):
    attn, ffn, grp = mesh.devices.shape
    cut = Mesh(mesh.devices.reshape(attn // 2, 2, ffn, grp), ATTN + ("ffn", "grp"))
    placed = (
        P(None, ATTN),
        P(ATTN),
        P(ATTN),
        P(ATTN, ("ffn", "grp")),
        P(ATTN, "ffn", None),
        P(("ffn", "grp"), ATTN),
        P(ATTN, None, ("ffn", "grp")),
        P(("ffn", "grp"), ATTN),
        P(ATTN, "ffn", "grp", None),
        P(),
        P(),
    )
    return jax.shard_map(
        shards, mesh=cut, in_specs=placed, out_specs=P(None, ATTN), check_vma=False
    )
```

```python
import jax
import jax.numpy as jnp
from jax import lax
from jax.sharding import Mesh
from jax.sharding import PartitionSpec as P

D = 8192
F32 = jnp.float32
BF16 = jnp.bfloat16


ATTN = ("chip", "core")


def exchange(parts, axis):
    return lax.all_to_all(parts, axis, 0, 0)


def spread(part, axis):
    count = lax.psum(1, axis)
    return exchange(jnp.broadcast_to(part[None], (count,) + part.shape), axis)


def angles(position, size):
    half = size // 2
    freqs = 500000.0 ** (-(jnp.arange(half, dtype=F32) * 2.0 / size))
    turned = position[:, None] * freqs[None, :]
    return jnp.cos(turned)[:, None, :], jnp.sin(turned)[:, None, :]


def rotate(values, cosine, sine):
    half = values.shape[-1] // 2
    first = values[..., :half]
    second = values[..., half:]
    return jnp.concatenate([first * cosine - second * sine, second * cosine + first * sine], -1)


def dot(a, b):
    return jnp.dot(a, b, preferred_element_type=F32)


def sum_relay(part, axis, ahead, behind, tied):
    def swap(values, pair):
        return lax.ppermute(values, axis, (pair, pair[::-1]))

    def hand(values, sources, targets):
        return lax.ppermute(values, axis, tuple(zip(sources, targets)))

    def add(one, two):
        return (one.astype(F32) + two.astype(F32)).astype(BF16)

    mine = part.astype(BF16)
    here = (lax.axis_index(axis) == ahead[0]) | (lax.axis_index(axis) == ahead[1])
    from_ahead = lax.cond(here, lambda values: swap(values, ahead), jnp.zeros_like, mine)
    sum_ahead = add(mine, from_ahead)
    down = hand(jnp.pad(sum_ahead, ((0, 16), (0, 0))), ahead, behind)[: part.shape[0]]
    mine = jnp.where(here, sum_ahead, mine)
    from_behind = lax.cond(here, jnp.zeros_like, lambda values: swap(values, behind), mine)
    sum_behind = add(mine, from_behind)
    sent = jnp.where(here, down, sum_behind) if tied else sum_behind
    up = hand(sent, behind, ahead)
    near = jnp.where(here, sum_ahead, sum_behind)
    far = jnp.where(here, up, down)
    return near.astype(F32) + far.astype(F32)


def sum_spread(part, axis):
    return jnp.sum(spread(part.astype(BF16), axis).astype(F32), 0)


def shards(
    layer_in,
    gain_attn,
    gain_ffn,
    w_query,
    w_keyval,
    w_out,
    w_gate_up,
    w_down,
    cache,
    cache_len,
    request_slot,
):
    requests = layer_in.shape[0]
    req_here = cache.shape[0]
    slots_here = cache.shape[2]
    head_size = cache.shape[3] // 2
    query_cols = w_query.shape[1]
    heads_mine = query_cols // head_size
    attn_count = lax.psum(1, ATTN)
    grp_count = lax.axis_size("grp")
    heads_all = heads_mine * grp_count
    scale = head_size ** (-0.5)
    order = jnp.arange(requests, dtype=jnp.int32)
    matches = request_slot[None, :] == order[:, None]
    slot_rows = dot(matches.astype(BF16), layer_in)
    squares = jnp.sum(slot_rows * slot_rows, axis=1)
    squares = spread(squares[None], ATTN)

    slot_length = jnp.sum(jnp.where(matches, cache_len[None, :], 0), axis=1)
    my_length = lax.dynamic_slice_in_dim(
        slot_length, lax.axis_index(ATTN) * req_here, req_here, 0
    )
    cosine, sine = angles(my_length.astype(F32), head_size)
    positions = lax.axis_index("grp") * slots_here + jnp.arange(slots_here, dtype=jnp.int32)
    valid = (positions[None, :] < my_length[:, None])[:, None, :]
    keys_here = cache[:, 0, :, :head_size]
    values_here = cache[:, 0, :, head_size:]
    weights = jnp.concatenate([w_query, w_keyval.reshape(w_keyval.shape[0], -1)], 1)
    squares, cosine, sine, valid, keys_here, values_here, weights = lax.optimization_barrier(
        (squares, cosine, sine, valid, keys_here, values_here, weights)
    )
    squares = jnp.sum(squares, (0, 1))
    normed = (slot_rows * lax.rsqrt(squares / D + 1e-05)[:, None] * gain_attn).astype(BF16)
    packed = dot(normed, weights)
    summed = exchange(packed.reshape(attn_count, req_here, -1), ATTN)
    summed = jnp.sum(summed, 0)
    queries = rotate(
        summed[:, :query_cols].reshape(req_here, heads_mine, head_size), cosine, sine
    )
    queries = queries.astype(BF16)
    new_key = rotate(summed[:, None, query_cols : query_cols + head_size], cosine, sine)
    new_key = new_key.astype(BF16)
    new_value = summed[:, query_cols + head_size :].astype(BF16).astype(F32)
    own = jnp.sum(queries.astype(F32) * new_key.astype(F32), -1) * scale
    flat_queries, new_value, own = lax.optimization_barrier(
        (queries.reshape(req_here, query_cols), new_value, own)
    )
    all_queries = spread(flat_queries, "grp")
    grouped = all_queries.reshape(grp_count, req_here, heads_mine, head_size)
    grouped = jnp.swapaxes(grouped, 0, 1).reshape(req_here, heads_all, head_size)

    scores = jnp.einsum("rgd,rjd->rgj", grouped, keys_here, preferred_element_type=F32) * scale
    scores = jnp.where(valid, scores, -1e30)
    top = jnp.max(scores, -1)
    weights = jnp.where(valid, jnp.exp(scores - top[..., None]), 0.0)
    total = jnp.sum(weights, -1)
    mixed = jnp.einsum(
        "rgj,rjd->rgd", weights.astype(BF16), values_here, preferred_element_type=F32
    )
    half = (req_here, heads_all, head_size // 2)
    packed = jnp.concatenate(
        [mixed, jnp.broadcast_to(top[..., None], half), jnp.broadcast_to(total[..., None], half)],
        -1,
    )
    packed = packed.reshape(req_here, grp_count, heads_mine, 2 * head_size)
    packed = exchange(jnp.swapaxes(packed, 0, 1), "grp")
    mixed = packed[..., :head_size]
    top = packed[..., head_size]
    total = packed[..., head_size + head_size // 2]
    best = jnp.maximum(jnp.max(top, 0), own)
    factor = jnp.exp(top - best)
    own_weight = jnp.exp(own - best)
    denom = jnp.sum(total * factor, 0) + own_weight
    attended = jnp.sum(mixed * factor[..., None], 0)
    attended = attended + own_weight[..., None] * new_value[:, None, :]
    attended = (attended / denom[..., None]).astype(BF16).reshape(req_here, query_cols)
    attended = spread(attended, ATTN).reshape(requests, query_cols)
    to_requests = (request_slot[:, None] == order[None, :]).astype(BF16)
    attended = dot(to_requests, attended).astype(BF16)
    resid = layer_in.astype(F32)
    projected = sum_spread(dot(attended, w_out), "grp")
    middle = (resid + sum_relay(projected, "ffn", (0, 1), (3, 2), True)).astype(BF16)

    middle_float = middle.astype(F32)
    squares = jnp.sum(middle_float * middle_float, axis=1)
    squares_high = squares.astype(BF16)
    squares_low = (squares - squares_high.astype(F32)).astype(BF16)
    units = w_gate_up.shape[2]
    both = dot((middle_float * gain_ffn).astype(BF16), w_gate_up.reshape(w_gate_up.shape[0], -1))
    core = lax.axis_index("core")
    lane = jnp.arange(128, dtype=jnp.int32)[None, :]
    tail = jnp.where(lane % 64 < 32, squares_high[:, None], squares_low[:, None])
    tail = jnp.where(lane // 64 == core, tail, jnp.zeros((), BF16))
    packed = jnp.concatenate([both.astype(BF16), tail], 1)
    packed = packed.reshape(attn_count // 2, 2, req_here, -1)
    kept = lax.dynamic_index_in_dim(packed, core, 1, False)
    given = lax.dynamic_index_in_dim(packed, 1 - core, 1, False)
    pair = kept.astype(F32) + lax.ppermute(given, "core", ((0, 1), (1, 0))).astype(F32)
    packed = exchange(pair.astype(BF16), "chip").astype(F32)
    summed = jnp.sum(packed, 0)
    squares = sum(summed[:, 2 * units + start] for start in (0, 32, 64, 96))
    summed = summed * lax.rsqrt(squares / D + 1e-05)[:, None]
    active = (jax.nn.silu(summed[:, :units]) * summed[:, units : 2 * units]).astype(BF16)
    active = spread(active, ATTN).reshape(requests, units)
    down = sum_spread(dot(active, w_down), "grp")
    return (middle_float + sum_relay(down, "ffn", (3, 2), (0, 1), False)).astype(BF16)


def solution(mesh):
    attn, ffn, grp = mesh.devices.shape
    cut = Mesh(mesh.devices.reshape(attn // 2, 2, ffn, grp), ATTN + ("ffn", "grp"))
    placed = (
        P(None, ATTN),
        P(ATTN),
        P(ATTN),
        P(ATTN, ("ffn", "grp")),
        P(ATTN, "ffn", None),
        P(("ffn", "grp"), ATTN),
        P(ATTN, None, ("ffn", "grp")),
        P(("ffn", "grp"), ATTN),
        P(ATTN, "ffn", "grp", None),
        P(),
        P(),
    )
    return jax.shard_map(
        shards, mesh=cut, in_specs=placed, out_specs=P(None, ATTN), check_vma=False
    )
```

```python
import jax
import jax.numpy as jnp
from jax import lax
from jax.sharding import Mesh
from jax.sharding import PartitionSpec as P

D = 8192
F32 = jnp.float32
BF16 = jnp.bfloat16


ATTN = ("chip", "core")


def exchange(parts, axis):
    return lax.all_to_all(parts, axis, 0, 0)


def spread(part, axis):
    count = lax.psum(1, axis)
    return exchange(jnp.broadcast_to(part[None], (count,) + part.shape), axis)


def angles(position, size):
    half = size // 2
    freqs = 500000.0 ** (-(jnp.arange(half, dtype=F32) * 2.0 / size))
    turned = position[:, None] * freqs[None, :]
    return jnp.cos(turned)[:, None, :], jnp.sin(turned)[:, None, :]


def rotate(values, cosine, sine):
    half = values.shape[-1] // 2
    first = values[..., :half]
    second = values[..., half:]
    return jnp.concatenate([first * cosine - second * sine, second * cosine + first * sine], -1)


def dot(a, b):
    return jnp.dot(a, b, preferred_element_type=F32)


def sum_relay(part, axis, ahead, behind, tied):
    def swap(values, pair):
        return lax.ppermute(values, axis, (pair, pair[::-1]))

    def hand(values, sources, targets):
        return lax.ppermute(values, axis, tuple(zip(sources, targets)))

    def add(one, two):
        return (one.astype(F32) + two.astype(F32)).astype(BF16)

    mine = part.astype(BF16)
    mine, place = lax.optimization_barrier((mine, lax.axis_index(axis)))
    here = (place == ahead[0]) | (place == ahead[1])
    if tied:
        from_ahead = swap(mine, ahead)
    else:
        from_ahead = lax.cond(here, lambda values: swap(values, ahead), jnp.zeros_like, mine)
    sum_ahead = add(mine, from_ahead)
    down = hand(jnp.pad(sum_ahead, ((0, 16), (0, 0))), ahead, behind)[: part.shape[0]]
    mine = jnp.where(here, sum_ahead, mine)
    if tied:
        from_behind = swap(mine, behind)
    else:
        from_behind = lax.cond(here, jnp.zeros_like, lambda values: swap(values, behind), mine)
    sum_behind = add(mine, from_behind)
    sent = jnp.where(here, down, sum_behind) if tied else sum_behind
    up = hand(sent, behind, ahead)
    near = jnp.where(here, sum_ahead, sum_behind)
    far = jnp.where(here, up, down)
    return near.astype(F32) + far.astype(F32)


def sum_spread(part, axis):
    return jnp.sum(spread(part.astype(BF16), axis).astype(F32), 0)


def shards(
    layer_in,
    gain_attn,
    gain_ffn,
    w_query,
    w_keyval,
    w_out,
    w_gate_up,
    w_down,
    cache,
    cache_len,
    request_slot,
):
    requests = layer_in.shape[0]
    req_here = cache.shape[0]
    slots_here = cache.shape[2]
    head_size = cache.shape[3] // 2
    query_cols = w_query.shape[1]
    heads_mine = query_cols // head_size
    attn_count = lax.psum(1, ATTN)
    grp_count = lax.axis_size("grp")
    heads_all = heads_mine * grp_count
    scale = head_size ** (-0.5)
    order = jnp.arange(requests, dtype=jnp.int32)
    matches = request_slot[None, :] == order[:, None]
    slot_rows = dot(matches.astype(BF16), layer_in)
    squares = jnp.sum(slot_rows * slot_rows, axis=1)
    squares = spread(squares[None], ATTN)

    slot_length = jnp.sum(jnp.where(matches, cache_len[None, :], 0), axis=1)
    my_length = lax.dynamic_slice_in_dim(
        slot_length, lax.axis_index(ATTN) * req_here, req_here, 0
    )
    cosine, sine = angles(my_length.astype(F32), head_size)
    positions = lax.axis_index("grp") * slots_here + jnp.arange(slots_here, dtype=jnp.int32)
    valid = (positions[None, :] < my_length[:, None])[:, None, :]
    keys_here = cache[:, 0, :, :head_size]
    values_here = cache[:, 0, :, head_size:]
    weights = jnp.concatenate([w_query, w_keyval.reshape(w_keyval.shape[0], -1)], 1)
    squares, cosine, sine, valid, keys_here, values_here, weights = lax.optimization_barrier(
        (squares, cosine, sine, valid, keys_here, values_here, weights)
    )
    squares = jnp.sum(squares, (0, 1))
    normed = (slot_rows * lax.rsqrt(squares / D + 1e-05)[:, None] * gain_attn).astype(BF16)
    packed = dot(normed, weights)
    summed = exchange(packed.reshape(attn_count, req_here, -1), ATTN)
    summed = jnp.sum(summed, 0)
    queries = rotate(
        summed[:, :query_cols].reshape(req_here, heads_mine, head_size), cosine, sine
    )
    queries = queries.astype(BF16)
    new_key = rotate(summed[:, None, query_cols : query_cols + head_size], cosine, sine)
    new_key = new_key.astype(BF16)
    new_value = summed[:, query_cols + head_size :].astype(BF16).astype(F32)
    own = jnp.sum(queries.astype(F32) * new_key.astype(F32), -1) * scale
    flat_queries, new_value, own = lax.optimization_barrier(
        (queries.reshape(req_here, query_cols), new_value, own)
    )
    all_queries = spread(flat_queries, "grp")
    grouped = all_queries.reshape(grp_count, req_here, heads_mine, head_size)
    grouped = jnp.swapaxes(grouped, 0, 1).reshape(req_here, heads_all, head_size)

    scores = jnp.einsum("rgd,rjd->rgj", grouped, keys_here, preferred_element_type=F32) * scale
    scores = jnp.where(valid, scores, -1e30)
    top = jnp.max(scores, -1)
    weights = jnp.where(valid, jnp.exp(scores - top[..., None]), 0.0)
    total = jnp.sum(weights, -1)
    mixed = jnp.einsum(
        "rgj,rjd->rgd", weights.astype(BF16), values_here, preferred_element_type=F32
    )
    half = (req_here, heads_all, head_size // 2)
    packed = jnp.concatenate(
        [mixed, jnp.broadcast_to(top[..., None], half), jnp.broadcast_to(total[..., None], half)],
        -1,
    )
    packed = packed.reshape(req_here, grp_count, heads_mine, 2 * head_size)
    packed = exchange(jnp.swapaxes(packed, 0, 1), "grp")
    mixed = packed[..., :head_size]
    top = packed[..., head_size]
    total = packed[..., head_size + head_size // 2]
    best = jnp.maximum(jnp.max(top, 0), own)
    factor = jnp.exp(top - best)
    own_weight = jnp.exp(own - best)
    denom = jnp.sum(total * factor, 0) + own_weight
    attended = jnp.sum(mixed * factor[..., None], 0)
    attended = attended + own_weight[..., None] * new_value[:, None, :]
    attended = (attended / denom[..., None]).astype(BF16).reshape(req_here, query_cols)
    attended = spread(attended, ATTN).reshape(requests, query_cols)
    to_requests = (request_slot[:, None] == order[None, :]).astype(BF16)
    attended = dot(to_requests, attended).astype(BF16)
    resid = layer_in.astype(F32)
    projected = sum_spread(dot(attended, w_out), "grp")
    middle = (resid + sum_relay(projected, "ffn", (0, 1), (3, 2), True)).astype(BF16)

    middle_float = middle.astype(F32)
    squares = jnp.sum(middle_float * middle_float, axis=1)
    squares_high = squares.astype(BF16)
    squares_low = (squares - squares_high.astype(F32)).astype(BF16)
    units = w_gate_up.shape[2]
    both = dot((middle_float * gain_ffn).astype(BF16), w_gate_up.reshape(w_gate_up.shape[0], -1))
    core = lax.axis_index("core")
    lane = jnp.arange(128, dtype=jnp.int32)[None, :]
    tail = jnp.where(lane % 64 < 32, squares_high[:, None], squares_low[:, None])
    tail = jnp.where(lane // 64 == core, tail, jnp.zeros((), BF16))
    packed = jnp.concatenate([both.astype(BF16), tail], 1)
    packed = packed.reshape(attn_count // 2, 2, req_here, -1)
    kept = lax.dynamic_index_in_dim(packed, core, 1, False)
    given = lax.dynamic_index_in_dim(packed, 1 - core, 1, False)
    pair = kept.astype(F32) + lax.ppermute(given, "core", ((0, 1), (1, 0))).astype(F32)
    packed = exchange(pair.astype(BF16), "chip").astype(F32)
    summed = jnp.sum(packed, 0)
    squares = sum(summed[:, 2 * units + start] for start in (0, 32, 64, 96))
    summed = summed * lax.rsqrt(squares / D + 1e-05)[:, None]
    active = (jax.nn.silu(summed[:, :units]) * summed[:, units : 2 * units]).astype(BF16)
    active = spread(active, ATTN).reshape(requests, units)
    down = sum_spread(dot(active, w_down), "grp")
    return (middle_float + sum_relay(down, "ffn", (3, 2), (0, 1), False)).astype(BF16)


def solution(mesh):
    attn, ffn, grp = mesh.devices.shape
    cut = Mesh(mesh.devices.reshape(attn // 2, 2, ffn, grp), ATTN + ("ffn", "grp"))
    placed = (
        P(None, ATTN),
        P(ATTN),
        P(ATTN),
        P(ATTN, ("ffn", "grp")),
        P(ATTN, "ffn", None),
        P(("ffn", "grp"), ATTN),
        P(ATTN, None, ("ffn", "grp")),
        P(("ffn", "grp"), ATTN),
        P(ATTN, "ffn", "grp", None),
        P(),
        P(),
    )
    return jax.shard_map(
        shards, mesh=cut, in_specs=placed, out_specs=P(None, ATTN), check_vma=False
    )
```
